32 devices in a mesh: curve: 16 (over z, y, x), colour: 2 (over core).
Axes of the slice: x: 2, y: 2, z: 4, core: 2. Of those that a mesh axis runs over, the one named last changes fastest.
Arguments:
- vectors: float32 [128, 320, 128], P(('curve', 'colour')), may hold values from -6 to 6
- inverse_blocks: bfloat16 [128, 320, 320], P(('curve', 'colour'))
- face_jac: float32 [128, 6, 5, 5, 16], P(('curve', 'colour')), may hold values from -2.64 to 2.64
- volume_jac: float32 [128, 3, 5, 5, 64], P(('curve', 'colour')), may hold values from -2.5 to 2.5
- neighbour_kind: int32 [128, 6], P(('curve', 'colour')), may hold values from 0 to 3, as said below
- neighbour_slot: int32 [128, 6], P(('curve', 'colour')), may hold values from 0 to 23
- hanging_face: int32 [128, 6], P(('curve', 'colour')), may hold values from 0 to 4
- send_upward: int32 [32], P(('curve', 'colour')), may hold values from 0 to 23, as said below
- send_downward: int32 [32], P(('curve', 'colour')), may hold values from 0 to 23
Outputs:
- preconditioned: float32 [128, 320, 128], P(('curve', 'colour'))
The draws below stay inside these ranges and needn't reach their ends.
Inputs may be any that keep to these rules, and one draw needn't show every extreme that they name: `neighbour_kind`: 0 marks a boundary face, 1 a neighbour on the same device, 2 one on the device before, 3 one on the device after. On every device, for each i < 1, the face named by send_upward entry i has kind 2 and neighbour_slot mod 1 equal to i, and the face named by send_downward entry i has kind 3 and neighbour_slot mod 1 equal to i. The 2 faces that one device names in send_upward and send_downward are all different.
All inputs are finite; a program needn't handle non-finite values.
Results may differ from the reference program's by a relative error of at most 0.0003.
Values sent between devices are 32-bit elements; how exact they have to be, the bound alone decides.
A program may use at most 192 MiB of HBM per device.

```python
import math
import jax
import jax.numpy as jnp
import numpy as np
from jax import lax

NP = 4
E_DEV = 4
NV = 128
SENDS = 1
BLOCK = 320
ELEMS = 128
N_CURVE = 16
N_COLOUR = 2


def face_layout(key):
    device_count = ELEMS // E_DEV
    face_count = 6 * E_DEV
    key_order, key_kind, key_slot, key_extra = jax.random.split(key, 4)
    scores = jax.random.randint(key_order, (device_count, face_count), 0, 1 << 20) * face_count + jnp.arange(face_count, dtype=jnp.int32)[None, :]
    face_order = jnp.argsort(scores, axis=1).astype(jnp.int32)
    face_rank = jnp.argsort(face_order, axis=1).astype(jnp.int32)
    base_kind = jax.random.randint(key_kind, (device_count, face_count), 0, 4).astype(jnp.int32)
    base_slot = jax.random.randint(key_slot, (device_count, face_count), 0, face_count).astype(jnp.int32)
    slot_extra = jax.random.randint(key_extra, (device_count, face_count), 0, face_count // SENDS).astype(jnp.int32)
    chosen = face_rank < 2 * SENDS
    kind_codes = jnp.where(face_rank < SENDS, 2, jnp.where(chosen, 3, base_kind)).astype(jnp.int32)
    slot_codes = jnp.where(chosen, face_rank % SENDS + SENDS * slot_extra, base_slot).astype(jnp.int32)
    upward = face_order[:, :SENDS].reshape(device_count * SENDS)
    downward = face_order[:, SENDS:2 * SENDS].reshape(device_count * SENDS)
    return (kind_codes.reshape(ELEMS, 6), slot_codes.reshape(ELEMS, 6), upward, downward, chosen.reshape(ELEMS, 6))


def draw_neighbour_kind(key, part):
    layout = face_layout(key)
    return layout[0]


def draw_neighbour_slot(key, part):
    layout = face_layout(key)
    return layout[1]


def draw_send_upward(key, part):
    layout = face_layout(key)
    return layout[2]


def draw_send_downward(key, part):
    layout = face_layout(key)
    return layout[3]


def draw_face_jac(key, part):
    layout = face_layout(key)
    key = jax.random.fold_in(key, 9)
    shape = (ELEMS, 6, 5, 5, NP * NP)
    scales = jnp.where(layout[4], 0.66, 0.12).astype(jnp.float32)[:, :, None, None, None]
    noise = jnp.clip(jax.random.normal(key, shape, jnp.float32), -4.0, 4.0)
    return (noise * scales).astype(jnp.float32)


def draw_inverse_blocks(key, part):
    key = jax.random.fold_in(key, 7)
    noise = jax.random.normal(key, (ELEMS, BLOCK, BLOCK), jnp.float32)
    diagonal = 0.6 * jnp.eye(BLOCK, dtype=jnp.float32)
    return (diagonal[None] + noise * (0.6 / math.sqrt(BLOCK))).astype(jnp.bfloat16)


def with_ends(values, own_key, least, high):
    dims = values.shape
    index_at = [jax.random.randint(jax.random.fold_in(own_key, axis), (), 0, dims[axis]) for axis in range(len(dims))]
    values = values.at[tuple(index_at)].set(least)
    longest = dims.index(max(dims))
    index_at[longest] = (index_at[longest] + 1) % dims[longest]
    return values.at[tuple(index_at)].set(high)


def shard_levels(key, extent, cuts, least, high):
    def one(dim, parts):
        steps = jax.random.uniform(jax.random.fold_in(jax.random.fold_in(key, 6), dim), (parts,), jnp.float32, least / len(cuts), high / len(cuts))
        return jnp.repeat(jnp.exp(steps), extent[dim] // parts).reshape((-1,) + (1,) * (len(extent) - dim - 1))

    level = one(*cuts[0])
    for cut in cuts[1:]:
        level = level * one(*cut)
    return level


def gaussian(rng, shape, spread, reach, shards=(), kind=jnp.bfloat16):
    factor_of = shard_levels(rng, shape, shards, -0.22, 0.18) if shards else 1.0
    values = jax.random.normal(rng, shape, jnp.float32) * spread * factor_of
    return jnp.minimum(jnp.maximum(values, -reach), reach).astype(kind)


def setup_inputs(seed: int = 0) -> dict:
    seeds = jax.random.split(jax.random.key(seed), 10)
    vectors = gaussian(seeds[0], (ELEMS, BLOCK, NV), 1.0, 6.0, ((0, 32),), jnp.float32)
    inverse_blocks = draw_inverse_blocks(jax.random.fold_in(seeds[9], 71), 0)
    face_jac = draw_face_jac(jax.random.fold_in(seeds[9], 71), 0)
    volume_jac = gaussian(seeds[3], (ELEMS, 3, 5, 5, NP ** 3), 0.3, 2.5, ((0, 32),), jnp.float32)
    neighbour_kind = draw_neighbour_kind(jax.random.fold_in(seeds[9], 71), 0)
    neighbour_slot = draw_neighbour_slot(jax.random.fold_in(seeds[9], 71), 0)
    hanging_face = with_ends(jax.random.randint(seeds[6], (ELEMS, 6), 0, 5), jax.random.fold_in(seeds[6], 1), 0, 4).astype(jnp.int32)
    send_upward = draw_send_upward(jax.random.fold_in(seeds[9], 71), 0)
    send_downward = draw_send_downward(jax.random.fold_in(seeds[9], 71), 0)
    return dict(vectors=vectors, inverse_blocks=inverse_blocks, face_jac=face_jac, volume_jac=volume_jac, neighbour_kind=neighbour_kind, neighbour_slot=neighbour_slot, hanging_face=hanging_face, send_upward=send_upward, send_downward=send_downward)


EXACT_PRODUCT = lax.Precision.HIGHEST

def edge_points(edge_count):
    return -np.cos(np.pi * np.arange(edge_count) / (edge_count - 1))

def lagrange_values(edge_nodes, points):
    values = np.ones((len(points), len(edge_nodes)))
    for j in range(len(edge_nodes)):
        for m in range(len(edge_nodes)):
            if m != j:
                values[:, j] = values[:, j] * (points - edge_nodes[m]) / (edge_nodes[j] - edge_nodes[m])
    return values

def lagrange_slopes(edge_nodes):
    point_count = len(edge_nodes)
    slopes = np.zeros((point_count, point_count))
    for i in range(point_count):
        for j in range(point_count):
            for m in range(point_count):
                if m != j:
                    product = 1.0 / (edge_nodes[j] - edge_nodes[m])
                    for k in range(point_count):
                        if k != j and k != m:
                            product = product * (edge_nodes[i] - edge_nodes[k]) / (edge_nodes[j] - edge_nodes[k])
                    slopes[i, j] = slopes[i, j] + product
    return slopes

def mortar_table(edge_count):
    edge_nodes = edge_points(edge_count)
    halves = [lagrange_values(edge_nodes, (edge_nodes - 1.0) / 2.0), lagrange_values(edge_nodes, (edge_nodes + 1.0) / 2.0)]
    tables = [np.eye(edge_count * edge_count)]
    for q in range(4):
        tables.append(np.kron(halves[q // 2], halves[q % 2]))
    return jnp.asarray(np.stack(tables), dtype=jnp.float32)

def slope_table(edge_count):
    return jnp.asarray(0.25 * lagrange_slopes(edge_points(edge_count)), dtype=jnp.float32)

def face_traces(field):
    elements, fields, edge_count, columns = (field.shape[0], field.shape[1], field.shape[2], field.shape[-1])
    last_node = edge_count - 1
    face_sides = [field[:, :, 0], field[:, :, last_node], field[:, :, :, 0], field[:, :, :, last_node], field[:, :, :, :, 0], field[:, :, :, :, last_node]]
    return jnp.stack([side_values.reshape(elements, fields, edge_count * edge_count, columns) for side_values in face_sides], axis=1)

def lift_faces(flux):
    elements, fields, square, columns = (flux.shape[0], flux.shape[2], flux.shape[3], flux.shape[4])
    edge_count = math.isqrt(square)
    last_node = edge_count - 1
    face_parts = flux.reshape(elements, 6, fields, edge_count, edge_count, columns)
    lifted = jnp.zeros((elements, fields, edge_count, edge_count, edge_count, columns), flux.dtype)
    lifted = lifted.at[:, :, 0].add(face_parts[:, 0])
    lifted = lifted.at[:, :, last_node].add(face_parts[:, 1])
    lifted = lifted.at[:, :, :, 0].add(face_parts[:, 2])
    lifted = lifted.at[:, :, :, last_node].add(face_parts[:, 3])
    lifted = lifted.at[:, :, :, :, 0].add(face_parts[:, 4])
    lifted = lifted.at[:, :, :, :, last_node].add(face_parts[:, 5])
    return lifted

def couple(traces, hanging, face_jac, mortar):
    choosers = (hanging[:, :, None] == jnp.arange(mortar.shape[0], dtype=jnp.int32)[None, None, :]).astype(traces.dtype)
    mortar_maps = jnp.einsum('esh,hnm->esnm', choosers, mortar.astype(traces.dtype), precision=EXACT_PRODUCT)
    mapped = jnp.einsum('esnm,esamk->esank', mortar_maps, traces, precision=EXACT_PRODUCT)
    return jnp.einsum('esabn,esbnk->esank', face_jac, mapped, precision=EXACT_PRODUCT)

def volume_term(field, volume_jac, slopes):
    elements, fields, edge_count, columns = (field.shape[0], field.shape[1], field.shape[2], field.shape[-1])
    flat_field = field.reshape(elements, fields, edge_count ** 3, columns)
    einsum_forms = ['ij,eajbck->eaibck', 'ij,eabjck->eabick', 'ij,eabcjk->eabcik']
    accumulated = jnp.zeros_like(field)
    for t in range(3):
        flux = jnp.einsum('eabp,ebpk->eapk', volume_jac[:, t], flat_field, precision=EXACT_PRODUCT).reshape(field.shape)
        accumulated = accumulated + jnp.einsum(einsum_forms[t], slopes.astype(field.dtype), flux, precision=EXACT_PRODUCT)
    return accumulated

def neighbour_rows(kind_codes, slot_codes, local_rows, sends):
    lower_row = local_rows + slot_codes % sends
    upper_row = local_rows + sends + slot_codes % sends
    empty_row = local_rows + 2 * sends
    return jnp.where(kind_codes == 1, slot_codes, jnp.where(kind_codes == 2, lower_row, jnp.where(kind_codes == 3, upper_row, empty_row)))

def apply_jacobian(field, lower_buffer, upper_buffer, volume_jac, face_jac, kind_codes, slot_codes, hanging, mortar, slopes):
    elements = field.shape[0]
    face_values = face_traces(field)
    flat_faces = face_values.reshape((elements * 6,) + face_values.shape[2:])
    trace_table = jnp.concatenate([flat_faces, lower_buffer, upper_buffer, jnp.zeros_like(lower_buffer[:1])], axis=0)
    row_index = neighbour_rows(kind_codes, slot_codes, elements * 6, lower_buffer.shape[0])
    gathered = jnp.take(trace_table, row_index, axis=0)
    return field + volume_term(field, volume_jac, slopes) + lift_faces(couple(gathered, hanging, face_jac, mortar))

def sweep(rhs, incoming, kind_codes, slot_codes, hanging, face_jac, inverse_blocks, mortar, backward):
    elements, columns = (rhs.shape[0], rhs.shape[-1])
    sends = incoming.shape[0]
    block_size = rhs[0].size // columns
    remote_kind = 3 if backward else 2

    def advance(position, solved):
        j = elements - 1 - position if backward else position
        face_values = face_traces(solved)
        flat_faces = face_values.reshape((elements * 6,) + face_values.shape[2:])
        trace_table = jnp.concatenate([flat_faces, incoming, jnp.zeros_like(incoming[:1])], axis=0)
        kind_row = lax.dynamic_index_in_dim(kind_codes, j, 0, keepdims=False)
        slot_row = lax.dynamic_index_in_dim(slot_codes, j, 0, keepdims=False)
        if backward:
            local_ok = (kind_row == 1) & (slot_row // 6 > j)
        else:
            local_ok = (kind_row == 1) & (slot_row // 6 < j)
        row_index = jnp.where(local_ok, slot_row, jnp.where(kind_row == remote_kind, elements * 6 + slot_row % sends, elements * 6 + sends))
        gathered = jnp.take(trace_table, row_index, axis=0)[None]
        hang_row = lax.dynamic_index_in_dim(hanging, j, 0, keepdims=True)
        jac_row = lax.dynamic_index_in_dim(face_jac, j, 0, keepdims=True)
        coupled = lift_faces(couple(gathered, hang_row, jac_row, mortar))[0].reshape(block_size, columns)
        inverse = lax.dynamic_index_in_dim(inverse_blocks, j, 0, keepdims=False).astype(rhs.dtype)
        own_values = lax.dynamic_index_in_dim(rhs, j, 0, keepdims=False).reshape(block_size, columns)
        if backward:
            updated = own_values - jnp.dot(inverse, coupled, precision=EXACT_PRODUCT)
        else:
            updated = jnp.dot(inverse, own_values - coupled, precision=EXACT_PRODUCT)
        return lax.dynamic_update_index_in_dim(solved, updated.reshape(rhs.shape[1:]), j, 0)
    return lax.fori_loop(0, elements, advance, jnp.zeros_like(rhs))

def reference(vectors, inverse_blocks, face_jac, volume_jac, neighbour_kind, neighbour_slot, hanging_face, send_upward, send_downward):
    devices = N_CURVE * N_COLOUR
    mortar = mortar_table(NP)
    slopes = slope_table(NP)
    square = NP * NP
    field = vectors.reshape(devices, E_DEV, 5, NP, NP, NP, NV)
    kind_codes = neighbour_kind.reshape(devices, E_DEV, 6)
    slot_codes = neighbour_slot.reshape(devices, E_DEV, 6)
    hanging = hanging_face.reshape(devices, E_DEV, 6)
    blocks = inverse_blocks.reshape(devices, E_DEV, BLOCK, BLOCK)
    face_jacs = face_jac.reshape(devices, E_DEV, 6, 5, 5, square)
    volume_jacs = volume_jac.reshape(devices, E_DEV, 3, 5, 5, NP ** 3)
    upward_lists = send_upward.reshape(devices, SENDS)
    downward_lists = send_downward.reshape(devices, SENDS)

    def buffers(inputs):
        local_field, upward_list, downward_list = inputs
        flat_faces = face_traces(local_field).reshape(E_DEV * 6, 5, square, NV)
        return (jnp.take(flat_faces, upward_list, axis=0), jnp.take(flat_faces, downward_list, axis=0))
    upward_bufs, downward_bufs = lax.map(buffers, (field, upward_lists, downward_lists))
    zero_buf = jnp.zeros_like(upward_bufs[:1])
    from_below = jnp.concatenate([zero_buf, upward_bufs[:-1]], axis=0)
    from_above = jnp.concatenate([downward_bufs[1:], zero_buf], axis=0)

    def jacobian_device(inputs):
        local_field, lower_buffer, upper_buffer, vjac_part, fjac_part, kind_part, slot_part, hang_part = inputs
        return apply_jacobian(local_field, lower_buffer, upper_buffer, vjac_part, fjac_part, kind_part, slot_part, hang_part, mortar, slopes)
    image = lax.map(jacobian_device, (field, from_below, from_above, volume_jacs, face_jacs, kind_codes, slot_codes, hanging))
    start = jnp.zeros((SENDS, 5, square, NV), vectors.dtype)

    def forward_step(incoming, inputs):
        rhs, kind_part, slot_part, hang_part, fjac_part, block_part, send_list = inputs
        solved = sweep(rhs, incoming, kind_part, slot_part, hang_part, fjac_part, block_part, mortar, False)
        flat_faces = face_traces(solved).reshape(E_DEV * 6, 5, square, NV)
        return (jnp.take(flat_faces, send_list, axis=0), solved)

    def backward_step(incoming, inputs):
        rhs, kind_part, slot_part, hang_part, fjac_part, block_part, send_list = inputs
        solved = sweep(rhs, incoming, kind_part, slot_part, hang_part, fjac_part, block_part, mortar, True)
        flat_faces = face_traces(solved).reshape(E_DEV * 6, 5, square, NV)
        return (jnp.take(flat_faces, send_list, axis=0), solved)
    carried, lowered = lax.scan(forward_step, start, (image, kind_codes, slot_codes, hanging, face_jacs, blocks, upward_lists))
    carried, result = lax.scan(backward_step, start, (lowered, kind_codes, slot_codes, hanging, face_jacs, blocks, downward_lists), reverse=True)
    return result.reshape(ELEMS, BLOCK, NV)
```

```python
import functools

import jax
import jax.numpy as jnp
import numpy as np
from jax import lax
from jax.experimental import pallas as pl
from jax.experimental.pallas import tpu as pltpu
from jax.sharding import PartitionSpec as P

NP = 4
F32 = jnp.float32
BF16 = jnp.bfloat16
AXES = ("curve", "colour")


def edge_points(edge_count):
    return -np.cos(np.pi * np.arange(edge_count) / (edge_count - 1))


def lagrange_values(edge_nodes, points):
    values = np.ones((len(points), len(edge_nodes)))
    for j in range(len(edge_nodes)):
        for m in range(len(edge_nodes)):
            if m != j:
                values[:, j] = (
                    values[:, j] * (points - edge_nodes[m]) / (edge_nodes[j] - edge_nodes[m])
                )
    return values


def lagrange_slopes(edge_nodes):
    point_count = len(edge_nodes)
    slopes = np.zeros((point_count, point_count))
    for i in range(point_count):
        for j in range(point_count):
            for m in range(point_count):
                if m != j:
                    product = 1.0 / (edge_nodes[j] - edge_nodes[m])
                    for k in range(point_count):
                        if k != j and k != m:
                            product = (
                                product
                                * (edge_nodes[i] - edge_nodes[k])
                                / (edge_nodes[j] - edge_nodes[k])
                            )
                    slopes[i, j] = slopes[i, j] + product
    return slopes


def mortar_tiles():
    edge_nodes = edge_points(NP)
    halves = [
        lagrange_values(edge_nodes, (edge_nodes - 1.0) / 2.0),
        lagrange_values(edge_nodes, (edge_nodes + 1.0) / 2.0),
    ]
    tables = [np.eye(NP * NP)]
    for q in range(4):
        tables.append(np.kron(halves[q // 2], halves[q % 2]))
    return np.tile(np.stack(tables), (1, 5, 15)).astype(np.float32)


def slope_tiles():
    d = 0.25 * lagrange_slopes(edge_points(NP))
    e = np.eye(NP)
    maps = [np.kron(np.kron(d, e), e), np.kron(np.kron(e, d), e), np.kron(np.kron(e, e), d)]
    return np.tile(np.stack(maps), (1, 1, 5)).astype(np.float32)


def split(x):
    high = x.astype(BF16)
    return high, (x - high.astype(F32)).astype(BF16)


def mm(a, b):
    return jnp.dot(a, b, preferred_element_type=F32)


def product(a, b):
    ah, al = split(a)
    bh, bl = split(b)
    return mm(ah, bh) + mm(ah, bl) + mm(al, bh)


def face_values(x, s, tmp):
    last = NP - 1 if s % 2 else 0
    if s < 2:
        return jnp.concatenate([x[pl.ds(f * 64 + last * 16, 16), :] for f in range(5)], axis=0)
    if s < 4:
        for c in range(4):
            tmp[pl.ds(c, 20, stride=4), :] = x[pl.ds(last * 4 + c, 20, stride=16), :]
        return tmp[...]
    return x[pl.ds(last, 80, stride=4), :]


def lift_into(acc, s, value, tmp):
    last = NP - 1 if s % 2 else 0
    if s < 2:
        for f in range(5):
            acc[pl.ds(f * 64 + last * 16, 16), :] += value[f * 16 : f * 16 + 16]
    elif s < 4:
        tmp[...] = value
        for c in range(4):
            acc[pl.ds(last * 4 + c, 20, stride=16), :] += tmp[pl.ds(c, 20, stride=4), :]
    else:
        acc[pl.ds(last, 80, stride=4), :] += value


def stacked(t):
    high, low = split(t)
    return jnp.concatenate([high, low, high], axis=0)


def pick_kernel(up_ref, down_ref, u_ref, out_ref, traces, tmp):
    for k, which in enumerate((up_ref, down_ref)):
        owner = which[0] // 6
        mine = u_ref.at[owner]
        for s in range(6):
            traces[s] = face_values(mine, s, tmp.at[s])
        out_ref[k] = traces[which[0] % 6]


def local_kernel(
    kind_ref,
    slot_ref,
    hang_ref,
    up_ref,
    down_ref,
    u_ref,
    inv_ref,
    jac_ref,
    vjac_ref,
    near_ref,
    mortar_ref,
    slope_ref,
    fwd_ref,
    bwd_ref,
    res_ref,
    maps,
    table_u,
    table_f,
    table_b,
    image,
    lowered,
    solved,
    acc,
    tmp,
):
    elements = u_ref.shape[0]
    rows = elements * 6
    lane = lax.broadcasted_iota(jnp.int32, (80, 240), 1)
    eye = (
        lax.broadcasted_iota(jnp.int32, (80, 128), 0)
        == lax.broadcasted_iota(jnp.int32, (80, 128), 1)
    ).astype(F32)
    none = jnp.zeros((240, 128), BF16)
    unit = stacked(eye)

    for j in range(elements):
        for s in range(6):
            wide = jac_ref[j * 6 + s] * mortar_ref[hang_ref[j, s]]
            high = wide.astype(BF16).astype(F32)
            maps[j * 6 + s] = jnp.where(lane < 160, high, wide - high).astype(BF16)
            table_u[j * 6 + s] = stacked(face_values(u_ref.at[j], s, tmp.at[s]))
    table_u[rows] = stacked(near_ref[0])
    table_u[rows + 1] = stacked(near_ref[1])
    table_u[rows + 2] = none
    for g in range(2):
        table_f[rows, :, g * 128 : g * 128 + 128] = unit if g == 1 else none
        table_f[rows + 1, :, g * 128 : g * 128 + 128] = none
    for g in range(3):
        table_b[rows, :, g * 128 : g * 128 + 128] = unit if g == 2 else none
        table_b[rows + 1, :, g * 128 : g * 128 + 128] = none

    for j in range(elements):
        parts = []
        for f in range(5):
            part = slope_ref[0] * vjac_ref[j, 0, f : f + 1, :]
            for t in range(1, 3):
                part = part + slope_ref[t] * vjac_ref[j, t, f : f + 1, :]
            parts.append(part)
        volume = jnp.concatenate(parts, axis=0)
        image[j] = u_ref[j] + product(volume, u_ref[j])
        for s in range(6):
            kind, slot = kind_ref[j, s], slot_ref[j, s]
            row = jnp.where(
                kind == 1, slot, jnp.where(kind == 2, rows, jnp.where(kind == 3, rows + 1, rows + 2))
            )
            lift_into(image.at[j], s, mm(maps[j * 6 + s], table_u[row]), tmp.at[s])

    for j in range(elements):
        acc[0] = jnp.zeros((320, 128), F32)
        acc[1] = jnp.zeros((320, 128), F32)
        for s in range(6):
            kind, slot = kind_ref[j, s], slot_ref[j, s]
            local = (kind == 1) & (slot < 6 * j)
            row = jnp.where(local, slot, jnp.where(kind == 2, rows, rows + 1))
            value = mm(maps[j * 6 + s], table_f[row])
            for g in range(2):
                lift_into(acc.at[g], s, value[:, g * 128 : g * 128 + 128], tmp.at[s * 3 + g])
        high, low = split(jnp.concatenate([image[j] - acc[0], -acc[1]], axis=1))
        value = mm(inv_ref[j], high) + mm(inv_ref[j], low)
        for g in range(2):
            lowered[g, j] = value[:, g * 128 : g * 128 + 128]
            for s in range(6):
                table_f[j * 6 + s, :, g * 128 : g * 128 + 128] = stacked(
                    face_values(lowered.at[g, j], s, tmp.at[s * 3 + g])
                )
    out = table_f[up_ref[0]]
    out = out[:80].astype(F32) + out[80:160].astype(F32)
    fwd_ref[0] = out[:, :128]
    fwd_ref[1] = out[:, 128:]

    for p in range(elements):
        j = elements - 1 - p
        for g in range(3):
            acc[g] = jnp.zeros((320, 128), F32)
        for s in range(6):
            kind, slot = kind_ref[j, s], slot_ref[j, s]
            local = (kind == 1) & (slot >= 6 * (j + 1))
            row = jnp.where(local, slot, jnp.where(kind == 3, rows, rows + 1))
            value = mm(maps[j * 6 + s], table_b[row])
            for g in range(3):
                lift_into(acc.at[g], s, value[:, g * 128 : g * 128 + 128], tmp.at[s * 3 + g])
        high, low = split(jnp.concatenate([acc[g] for g in range(3)], axis=1))
        value = mm(inv_ref[j], high) + mm(inv_ref[j], low)
        for g in range(3):
            part = value[:, g * 128 : g * 128 + 128]
            solved[g, j] = lowered[g, j] - part if g < 2 else -part
            res_ref[j, :, g * 128 : g * 128 + 128] = solved[g, j]
            for s in range(6):
                table_b[j * 6 + s, :, g * 128 : g * 128 + 128] = stacked(
                    face_values(solved.at[g, j], s, tmp.at[s * 3 + g])
                )
    out = table_b[down_ref[0]]
    out = out[:80].astype(F32) + out[80:160].astype(F32)
    for g in range(3):
        bwd_ref[g] = out[:, g * 128 : g * 128 + 128]


def scan_rounds(count):
    first = min(3, max(count - 1, 1))
    rounds, cover = [list(range(1, first + 1))], first
    while cover < count - 1:
        radix = 4 if cover * 3 < count - 1 else (3 if cover * 2 < count - 1 else 2)
        rounds.append([cover * i for i in range(1, radix)])
        cover *= radix
    return rounds


def scan_kernel(
    curve_size,
    colour_size,
    fwd_ref,
    bwd_ref,
    res_ref,
    out_ref,
    state_f,
    state_m,
    state_c,
    recv_f,
    recv_m,
    recv_c,
    both,
    send_sems,
    recv_sems,
):
    count = curve_size * colour_size
    rounds = scan_rounds(count)
    width = max(len(r) for r in rounds)
    me = lax.axis_index("curve") * colour_size + lax.axis_index("colour")

    def at(offset):
        other = lax.rem(me + offset + count, count)
        return (other // colour_size, lax.rem(other, colour_size))

    barrier = pltpu.get_barrier_semaphore()
    greeted = 0
    for offset in sorted({o for r in rounds for o in r}):
        for signed, there in ((offset, me + offset < count), (-offset, me >= offset)):
            greeted = greeted + there.astype(jnp.int32)

            @pl.when(there)
            def _():
                pl.semaphore_signal(
                    barrier, inc=1, device_id=at(signed), device_id_type=pl.DeviceIdType.MESH
                )

    pl.semaphore_wait(barrier, greeted)

    def exchange(kind, k, i, upward, source, target):
        offset = rounds[k][i]
        has_to = me + offset < count if upward else me >= offset
        has_from = me >= offset if upward else me + offset < count
        copy = pltpu.make_async_remote_copy(
            src_ref=source,
            dst_ref=target,
            send_sem=send_sems.at[kind, k, i],
            recv_sem=recv_sems.at[kind, k, i],
            device_id=at(offset if upward else -offset),
            device_id_type=pl.DeviceIdType.MESH,
        )

        @pl.when(has_to)
        def _():
            copy.start()

        @pl.when(jnp.logical_not(has_from))
        def _():
            target[...] = jnp.zeros(target.shape, F32)

        return copy, has_to, has_from

    sent = []

    def arrive(copies):
        for copy, has_to, has_from in copies:
            sent.append((copy, has_to))

            @pl.when(has_from)
            def _(copy=copy):
                copy.wait_recv()

    def compose(first, second):
        value = product(first[1][:, :80], jnp.concatenate([second[0], second[1]], axis=1))
        return (first[0] + value[:, :128], value[:, 128:])

    state_f[0] = fwd_ref[...]
    state_m[0] = bwd_ref[2]
    for k, offsets in enumerate(rounds):
        final = k == len(rounds) - 1
        copies = []
        for i in range(len(offsets)):
            copies.append(exchange(0, k, i, True, state_f.at[k], recv_f.at[k, i]))
            copies.append(exchange(1, k, i, False, state_m.at[k], recv_m.at[k, i]))
        arrive(copies)
        chain = [(recv_f[k, i, 0], recv_f[k, i, 1]) for i in range(len(offsets))]
        chain_m = [recv_m[k, i] for i in range(len(offsets))]
        if k > 0:
            chain = [(state_f[k, 0], state_f[k, 1])] + chain
            chain_m = [state_m[k]] + chain_m
        total = chain[-1]
        for item in chain[-2::-1]:
            total = compose(item, total)
        state_f[k + 1, 0] = total[0]
        if not final:
            state_f[k + 1, 1] = total[1]
            total_m = chain_m[-1]
            for item in chain_m[-2::-1]:
                total_m = product(item[:, :80], total_m)
            state_m[k + 1] = total_m

    incoming = state_f[len(rounds), 0]
    both[...] = jnp.zeros(both.shape, F32)
    both[0:80] = incoming
    state_c[0] = bwd_ref[0] + product(bwd_ref[1][:, :80], incoming)
    for k, offsets in enumerate(rounds):
        copies = [
            exchange(2, k, i, False, state_c.at[k], recv_c.at[k, i]) for i in range(len(offsets))
        ]
        arrive(copies)
        chain = [(recv_c[k, i], recv_m.at[k, i]) for i in range(len(offsets))]
        if k > 0:
            chain = [(state_c[k], state_m.at[k])] + chain
        total = chain[-1][0]
        for value, factor in chain[-2::-1]:
            total = value + product(factor[...][:, :80], total)
        state_c[k + 1] = total
    both[128:208] = state_c[len(rounds)]

    high, low = split(both[...])
    for j in range(out_ref.shape[0]):
        wh, wl = split(res_ref[j, :, 128:384])
        out_ref[j] = res_ref[j, :, 0:128] + mm(wh, high) + mm(wh, low) + mm(wl, high)
    for copy, has_to in sent:

        @pl.when(has_to)
        def _(copy=copy):
            copy.wait_send()


def on_device(
    curve_size,
    colour_size,
    vectors,
    inverse_blocks,
    face_jac,
    volume_jac,
    neighbour_kind,
    neighbour_slot,
    hanging_face,
    send_upward,
    send_downward,
):
    elements = vectors.shape[0]
    rows = elements * 6
    count = curve_size * colour_size
    rounds = scan_rounds(count)
    width = max(len(r) for r in rounds)
    smem = pl.BlockSpec(memory_space=pltpu.SMEM)
    vmem = pl.BlockSpec(memory_space=pltpu.VMEM)
    limit = 56 * 1024 * 1024

    near = pl.pallas_call(
        pick_kernel,
        out_shape=jax.ShapeDtypeStruct((2, 80, 128), F32),
        in_specs=[smem, smem, vmem],
        out_specs=vmem,
        scratch_shapes=[pltpu.VMEM((6, 80, 128), F32), pltpu.VMEM((6, 80, 128), F32)],
        compiler_params=pltpu.CompilerParams(vmem_limit_bytes=limit),
        name="pick",
    )(send_upward, send_downward, vectors)
    below = lax.ppermute(near[0], AXES, [(i, i + 1) for i in range(count - 1)])
    above = lax.ppermute(near[1], AXES, [(i + 1, i) for i in range(count - 1)])

    jac_wide = jnp.transpose(face_jac, (0, 1, 2, 4, 3)).reshape(rows, 80, 5)
    jac_wide = jnp.tile(jnp.repeat(jac_wide, 16, axis=2), (1, 1, 3))
    fwd, bwd, res = pl.pallas_call(
        local_kernel,
        out_shape=(
            jax.ShapeDtypeStruct((2, 80, 128), F32),
            jax.ShapeDtypeStruct((3, 80, 128), F32),
            jax.ShapeDtypeStruct((elements, 320, 384), F32),
        ),
        in_specs=[smem] * 5 + [vmem] * 7,
        out_specs=(vmem, vmem, vmem),
        scratch_shapes=[
            pltpu.VMEM((rows, 80, 240), BF16),
            pltpu.VMEM((rows + 3, 240, 128), BF16),
            pltpu.VMEM((rows + 2, 240, 256), BF16),
            pltpu.VMEM((rows + 2, 240, 384), BF16),
            pltpu.VMEM((elements, 320, 128), F32),
            pltpu.VMEM((2, elements, 320, 128), F32),
            pltpu.VMEM((3, elements, 320, 128), F32),
            pltpu.VMEM((3, 320, 128), F32),
            pltpu.VMEM((18, 80, 128), F32),
        ],
        compiler_params=pltpu.CompilerParams(vmem_limit_bytes=limit),
        name="local",
    )(
        neighbour_kind,
        neighbour_slot,
        hanging_face,
        send_upward,
        send_downward,
        vectors,
        inverse_blocks,
        jac_wide,
        volume_jac.reshape(elements, 3, 5, 320),
        jnp.stack([below, above]),
        jnp.asarray(mortar_tiles()),
        jnp.asarray(slope_tiles()),
    )
    depth = len(rounds)
    return pl.pallas_call(
        functools.partial(scan_kernel, curve_size, colour_size),
        out_shape=jax.ShapeDtypeStruct(vectors.shape, F32),
        in_specs=[vmem] * 3,
        out_specs=vmem,
        scratch_shapes=[
            pltpu.VMEM((depth + 1, 2, 80, 128), F32),
            pltpu.VMEM((depth + 1, 80, 128), F32),
            pltpu.VMEM((depth + 1, 80, 128), F32),
            pltpu.VMEM((depth, width, 2, 80, 128), F32),
            pltpu.VMEM((depth, width, 80, 128), F32),
            pltpu.VMEM((depth, width, 80, 128), F32),
            pltpu.VMEM((256, 128), F32),
            pltpu.SemaphoreType.DMA((3, depth, width)),
            pltpu.SemaphoreType.DMA((3, depth, width)),
        ],
        compiler_params=pltpu.CompilerParams(
            vmem_limit_bytes=limit, collective_id=0, has_side_effects=True
        ),
        name="scan",
    )(fwd, bwd, res)


def solution(mesh):
    split_first = lambda rank: P(AXES, *([None] * (rank - 1)))
    return jax.shard_map(
        functools.partial(on_device, mesh.shape["curve"], mesh.shape["colour"]),
        mesh=mesh,
        in_specs=tuple(split_first(r) for r in (3, 3, 5, 5, 2, 2, 2, 1, 1)),
        out_specs=split_first(3),
        check_vma=False,
    )
```

```python
import functools

import jax
import jax.numpy as jnp
import numpy as np
from jax import lax
from jax.experimental import pallas as pl
from jax.experimental.pallas import tpu as pltpu
from jax.sharding import PartitionSpec as P

NP = 4
F32 = jnp.float32
BF16 = jnp.bfloat16
AXES = ("curve", "colour")


def edge_points(edge_count):
    return -np.cos(np.pi * np.arange(edge_count) / (edge_count - 1))


def lagrange_values(edge_nodes, points):
    values = np.ones((len(points), len(edge_nodes)))
    for j in range(len(edge_nodes)):
        for m in range(len(edge_nodes)):
            if m != j:
                values[:, j] = (
                    values[:, j] * (points - edge_nodes[m]) / (edge_nodes[j] - edge_nodes[m])
                )
    return values


def lagrange_slopes(edge_nodes):
    point_count = len(edge_nodes)
    slopes = np.zeros((point_count, point_count))
    for i in range(point_count):
        for j in range(point_count):
            for m in range(point_count):
                if m != j:
                    product = 1.0 / (edge_nodes[j] - edge_nodes[m])
                    for k in range(point_count):
                        if k != j and k != m:
                            product = (
                                product
                                * (edge_nodes[i] - edge_nodes[k])
                                / (edge_nodes[j] - edge_nodes[k])
                            )
                    slopes[i, j] = slopes[i, j] + product
    return slopes


def mortar_tiles():
    edge_nodes = edge_points(NP)
    halves = [
        lagrange_values(edge_nodes, (edge_nodes - 1.0) / 2.0),
        lagrange_values(edge_nodes, (edge_nodes + 1.0) / 2.0),
    ]
    tables = [np.eye(NP * NP)]
    for q in range(4):
        tables.append(np.kron(halves[q // 2], halves[q % 2]))
    return np.tile(np.stack(tables), (1, 5, 15)).astype(np.float32)


def slope_tiles():
    d = 0.25 * lagrange_slopes(edge_points(NP))
    e = np.eye(NP)
    maps = [np.kron(np.kron(d, e), e), np.kron(np.kron(e, d), e), np.kron(np.kron(e, e), d)]
    return np.tile(np.stack(maps), (1, 1, 5)).astype(np.float32)


def split(x):
    high = x.astype(BF16)
    return high, (x - high.astype(F32)).astype(BF16)


def mm(a, b):
    return jnp.dot(a, b, preferred_element_type=F32)


def product(a, b):
    ah, al = split(a)
    bh, bl = split(b)
    return mm(ah, bh) + mm(ah, bl) + mm(al, bh)


def face_values(x, s, tmp):
    last = NP - 1 if s % 2 else 0
    if s < 2:
        return jnp.concatenate([x[pl.ds(f * 64 + last * 16, 16), :] for f in range(5)], axis=0)
    if s < 4:
        for c in range(4):
            tmp[pl.ds(c, 20, stride=4), :] = x[pl.ds(last * 4 + c, 20, stride=16), :]
        return tmp[...]
    return x[pl.ds(last, 80, stride=4), :]


def lift_into(acc, s, value, tmp):
    last = NP - 1 if s % 2 else 0
    if s < 2:
        for f in range(5):
            acc[pl.ds(f * 64 + last * 16, 16), :] += value[f * 16 : f * 16 + 16]
    elif s < 4:
        tmp[...] = value
        for c in range(4):
            acc[pl.ds(last * 4 + c, 20, stride=16), :] += tmp[pl.ds(c, 20, stride=4), :]
    else:
        acc[pl.ds(last, 80, stride=4), :] += value


def stacked(t):
    high, low = split(t)
    return jnp.concatenate([high, low, high], axis=0)


def scan_rounds(count):
    if count == 1:
        return []
    first = min(3, count - 1)
    rounds, cover = [list(range(1, first + 1))], first
    while cover < count - 1:
        radix = 4 if cover * 3 < count - 1 else (3 if cover * 2 < count - 1 else 2)
        rounds.append([cover * i for i in range(1, radix)])
        cover *= radix
    return rounds


def group_size(count):
    return next(size for size in (8, 4, 2, 1) if count % size == 0)


def kernel(
    curve_size,
    colour_size,
    kind_ref,
    slot_ref,
    hang_ref,
    up_ref,
    down_ref,
    u_ref,
    inv_ref,
    jac_ref,
    vjac_ref,
    mortar_ref,
    slope_ref,
    out_ref,
    maps,
    traces,
    leaving,
    near,
    table_u,
    table_wf,
    table_wb,
    table_y,
    table_z,
    image,
    wide_f,
    wide_b,
    lowered,
    solved,
    acc,
    tmp,
    group_m,
    group_v,
    factors,
    state_m,
    recv_m,
    state_v,
    recv_v,
    both,
    near_send,
    near_recv,
    group_send,
    group_recv,
    chain_send,
    chain_recv,
):
    elements = u_ref.shape[0]
    rows = elements * 6
    count = curve_size * colour_size
    size = group_size(count)
    rounds = scan_rounds(count // size)
    me = lax.axis_index("curve") * colour_size + lax.axis_index("colour")
    place = lax.rem(me, size)
    first = me - place

    def coordinates(other):
        other = lax.rem(other + count, count)
        return (other // colour_size, lax.rem(other, colour_size))

    barrier = pltpu.get_barrier_semaphore()
    greeted = jnp.int32(size - 1)

    def greet(other):
        pl.semaphore_signal(
            barrier, inc=1, device_id=coordinates(other), device_id_type=pl.DeviceIdType.MESH
        )

    def peer(i):
        return first + lax.rem(place + i, size)

    for i in range(1, size):
        greet(peer(i))
    distant = [
        (me + 1, (place == size - 1) & (me + 1 < count)),
        (me - 1, (place == 0) & (me > 0)),
    ]
    for offset in sorted({o for r in rounds for o in r}):
        if offset * size > 1:
            distant.append((me + offset * size, me + offset * size < count))
            distant.append((me - offset * size, me >= offset * size))
    for other, there in distant:
        greeted = greeted + there.astype(jnp.int32)

        @pl.when(there)
        def _(other=other):
            greet(other)

    sent = []

    def remote(source, target, send, recv, other, has_to, has_from):
        copy = pltpu.make_async_remote_copy(
            src_ref=source,
            dst_ref=target,
            send_sem=send,
            recv_sem=recv,
            device_id=coordinates(other),
            device_id_type=pl.DeviceIdType.MESH,
        )

        @pl.when(has_to)
        def _():
            copy.start()

        @pl.when(jnp.logical_not(has_from))
        def _():
            target[...] = jnp.zeros(target.shape, F32)

        sent.append((copy, has_to))
        return copy, has_from

    def arrive(copies):
        for copy, has_from in copies:

            @pl.when(has_from)
            def _(copy=copy):
                copy.wait_recv()

    lane = lax.broadcasted_iota(jnp.int32, (80, 240), 1)
    eye = (
        lax.broadcasted_iota(jnp.int32, (80, 128), 0)
        == lax.broadcasted_iota(jnp.int32, (80, 128), 1)
    ).astype(F32)
    none = jnp.zeros((240, 128), BF16)
    spread = (
        lax.rem(lax.broadcasted_iota(jnp.int32, (5, 240), 1), 80) // 16
        == lax.broadcasted_iota(jnp.int32, (5, 240), 0)
    ).astype(BF16)
    for j in range(elements):
        for s in range(6):
            t = face_values(u_ref.at[j], s, tmp.at[s])
            traces[j * 6 + s] = t
            table_u[j * 6 + s] = stacked(t)
    table_u[rows] = none
    leaving[0] = traces[up_ref[0]]
    leaving[1] = traces[down_ref[0]]
    pl.semaphore_wait(barrier, greeted)
    after, before = me + 1 < count, me > 0
    near_copies = [
        remote(leaving.at[0], near.at[0], near_send.at[0], near_recv.at[0], me + 1, after, before),
        remote(leaving.at[1], near.at[1], near_send.at[1], near_recv.at[1], me - 1, before, after),
    ]
    for j in range(elements):
        for s in range(6):
            high, low = split(jac_ref[j * 6 + s])
            wide = (mm(high, spread) + mm(low, spread)) * mortar_ref[hang_ref[j, s]]
            high = wide.astype(BF16).astype(F32)
            maps[j * 6 + s] = jnp.where(lane < 160, high, wide - high).astype(BF16)

    def step(j, backward, table, remote_row, empty_row, accs, tmps, own, dests):
        groups = len(dests)
        for g in range(groups):
            acc[accs + g] = jnp.zeros((320, 128), F32)
        for s in range(6):
            kind, slot = kind_ref[j, s], slot_ref[j, s]
            inside = slot >= 6 * (j + 1) if backward else slot < 6 * j
            row = jnp.where(kind == (3 if backward else 2), remote_row, empty_row)
            row = jnp.where((kind == 1) & inside, slot, row)
            value = mm(maps[j * 6 + s], table[row])
            for g in range(groups):
                lift_into(
                    acc.at[accs + g], s, value[:, g * 128 : g * 128 + 128], tmp.at[tmps + 6 * g + s]
                )
        if backward:
            right = [acc[accs + g] for g in range(groups)]
        else:
            right = [own[g] - acc[accs + g] for g in range(groups)]
        high, low = split(jnp.concatenate(right, axis=1) if groups > 1 else right[0])
        value = mm(inv_ref[j], high) + mm(inv_ref[j], low)
        for g in range(groups):
            part = value[:, g * 128 : g * 128 + 128]
            dests[g][...] = own[g] - part if backward else part
            for s in range(6):
                table[j * 6 + s, :, g * 128 : g * 128 + 128] = stacked(
                    face_values(dests[g], s, tmp.at[tmps + 6 * g + s])
                )

    def outgoing(table, which):
        out = table[which]
        return out[:80].astype(F32) + out[80:160].astype(F32)

    def share(buffer, kind):
        copies = []
        for i in range(1, size):
            copy = pltpu.make_async_remote_copy(
                src_ref=buffer.at[place],
                dst_ref=buffer.at[place],
                send_sem=group_send.at[kind, i],
                recv_sem=group_recv.at[kind, place],
                device_id=coordinates(peer(i)),
                device_id_type=pl.DeviceIdType.MESH,
            )
            copy.start()
            sent.append((copy, None))
        for i in range(1, size):
            other = lax.rem(place + i, size)
            copies.append(
                pltpu.make_async_remote_copy(
                    src_ref=buffer.at[other],
                    dst_ref=buffer.at[other],
                    send_sem=group_send.at[kind, i],
                    recv_sem=group_recv.at[kind, other],
                    device_id=coordinates(peer(i)),
                    device_id_type=pl.DeviceIdType.MESH,
                )
            )
        return copies

    unit = stacked(eye)
    for table in (table_wf, table_wb):
        table[rows] = unit
        table[rows + 1] = none
    zero = jnp.zeros((320, 128), F32)
    for p in range(elements):
        q = elements - 1 - p
        step(p, False, table_wf, rows, rows + 1, 0, 0, [zero], [wide_f.at[p]])
        step(q, True, table_wb, rows, rows + 1, 1, 6, [zero], [wide_b.at[q]])
    group_m[0, place] = outgoing(table_wf, up_ref[0])
    group_m[1, place] = outgoing(table_wb, down_ref[0])
    shared_m = [share(group_m.at[0], 0), share(group_m.at[1], 1)]

    arrive(near_copies)
    table_u[rows + 1] = stacked(near[0])
    table_u[rows + 2] = stacked(near[1])
    for j in range(elements):
        parts = []
        for f in range(5):
            part = slope_ref[0] * vjac_ref[j, 0, f : f + 1, :]
            for t in range(1, 3):
                part = part + slope_ref[t] * vjac_ref[j, t, f : f + 1, :]
            parts.append(part)
        volume = jnp.concatenate(parts, axis=0)
        image[j] = u_ref[j] + product(volume, u_ref[j])
        for s in range(6):
            kind, slot = kind_ref[j, s], slot_ref[j, s]
            row = jnp.where(kind == 1, slot, jnp.where(kind == 0, rows, rows + kind - 1))
            lift_into(image.at[j], s, mm(maps[j * 6 + s], table_u[row]), tmp.at[s])
    table_y[rows] = none
    for j in range(elements):
        step(j, False, table_y, rows, rows, 0, 0, [image[j]], [lowered.at[j]])
    group_v[0, place] = outgoing(table_y, up_ref[0])
    shared_f = share(group_v.at[0], 2)

    for copies in shared_m:
        for copy in copies:
            copy.wait_recv()
    chains = [jnp.concatenate([eye, eye], axis=0)] * 2
    for step_index in range(size):
        for way in range(2):
            e = step_index if way else size - 1 - step_index
            mine = place < e if way else place > e
            high, low = split(jnp.concatenate([jnp.where(mine, chains[way][:80], 0.0), chains[way][80:]], 0))
            factors[way, e, 0] = high
            factors[way, e, 1] = low
            m = group_m[way, e]
            mh, ml = split(m)
            full = chains[way][:, :80]
            ch, cl = split(full)
            following = mm(ch, mh) + mm(ch, ml) + mm(cl, mh)
            chains[way] = jnp.concatenate([jnp.where(mine, following[:80], eye), following[80:]], 0)
    enter = [chain[:80] for chain in chains]
    state_m[0, 0] = chains[0][80:]
    state_m[1, 0] = chains[1][80:]

    def pass_on(way, k, i, source, target, kind):
        offset = rounds[k][i] * size
        below, above = me >= offset, me + offset < count
        return remote(
            source,
            target,
            chain_send.at[kind, k, i],
            chain_recv.at[kind, k, i],
            me - offset if way else me + offset,
            below if way else above,
            above if way else below,
        )

    def start_m(k):
        return [
            pass_on(way, k, i, state_m.at[way, k], recv_m.at[way, k, i], way)
            for i in range(len(rounds[k]))
            for way in range(2)
        ]

    pending = start_m(0) if rounds else []

    table_z[rows, :, 0:128] = none
    table_z[rows, :, 128:256] = none
    for p in range(elements):
        q = elements - 1 - p
        step(
            q,
            True,
            table_z,
            rows,
            rows,
            0,
            0,
            [lowered[q], wide_f[q]],
            [solved.at[0, q], solved.at[1, q]],
        )
    back = outgoing(table_z, down_ref[0])

    for k in range(len(rounds)):
        arrive(pending)
        if k + 1 < len(rounds):
            for way in range(2):
                factor = [recv_m[way, k, i] for i in range(len(rounds[k]))]
                if k > 0:
                    factor = [state_m[way, k]] + factor
                total = factor[-1]
                for item in factor[-2::-1]:
                    total = product(item[:, :80], total)
                state_m[way, k + 1] = total
            pending = start_m(k + 1)

    def scan(way, copies):
        for copy in copies:
            copy.wait_recv()
        total = jnp.zeros((160, 128), F32)
        for e in range(size):
            high, low = split(group_v[way, e])
            fh, fl = factors[way, e, 0][:, :80], factors[way, e, 1][:, :80]
            total = total + mm(fh, high) + mm(fh, low) + mm(fl, high)
        if not rounds:
            return total[:80]
        state_v[way, 0] = total[80:]
        for k, offsets in enumerate(rounds):
            arrive(
                [
                    pass_on(way, k, i, state_v.at[way, k], recv_v.at[way, k, i], 2 + way)
                    for i in range(len(offsets))
                ]
            )
            links = [(recv_v.at[way, k, i], recv_m.at[way, k, i]) for i in range(len(offsets))]
            if k > 0:
                links = [(state_v.at[way, k], state_m.at[way, k])] + links
            value = links[-1][0][...]
            for term, factor in links[-2::-1]:
                value = term[...] + product(factor[:, :80], value)
            state_v[way, k + 1] = value
        return total[:80] + product(enter[way][:, :80], state_v[way, len(rounds)])

    both[...] = jnp.zeros(both.shape, F32)
    incoming = scan(0, shared_f)
    group_v[1, place] = back[:, :128] + product(back[:, 128:208], incoming)
    shared_b = share(group_v.at[1], 3)
    both[0:80] = incoming
    both[128:208] = scan(1, shared_b)

    high, low = split(both[...])
    for j in range(elements):
        wh, wl = split(jnp.concatenate([solved[1, j], wide_b[j]], axis=1))
        out_ref[j] = solved[0, j] + mm(wh, high) + mm(wh, low) + mm(wl, high)
    for copy, has_to in sent:
        if has_to is None:
            copy.wait_send()
        else:

            @pl.when(has_to)
            def _(copy=copy):
                copy.wait_send()


def on_device(
    curve_size,
    colour_size,
    vectors,
    inverse_blocks,
    face_jac,
    volume_jac,
    neighbour_kind,
    neighbour_slot,
    hanging_face,
    send_upward,
    send_downward,
):
    elements = vectors.shape[0]
    rows = elements * 6
    count = curve_size * colour_size
    size = group_size(count)
    rounds = scan_rounds(count // size)
    depth = max(len(rounds), 1)
    width = max([len(r) for r in rounds] + [1])
    smem = pl.BlockSpec(memory_space=pltpu.SMEM)
    vmem = pl.BlockSpec(memory_space=pltpu.VMEM)
    face = (80, 128)
    return pl.pallas_call(
        functools.partial(kernel, curve_size, colour_size),
        out_shape=jax.ShapeDtypeStruct(vectors.shape, F32),
        in_specs=[smem] * 5 + [vmem] * 6,
        out_specs=vmem,
        scratch_shapes=[
            pltpu.VMEM((rows, 80, 240), BF16),
            pltpu.VMEM((rows,) + face, F32),
            pltpu.VMEM((2,) + face, F32),
            pltpu.VMEM((2,) + face, F32),
            pltpu.VMEM((rows + 3, 240, 128), BF16),
            pltpu.VMEM((rows + 2, 240, 128), BF16),
            pltpu.VMEM((rows + 2, 240, 128), BF16),
            pltpu.VMEM((rows + 1, 240, 128), BF16),
            pltpu.VMEM((rows + 1, 240, 256), BF16),
            pltpu.VMEM((elements, 320, 128), F32),
            pltpu.VMEM((elements, 320, 128), F32),
            pltpu.VMEM((elements, 320, 128), F32),
            pltpu.VMEM((elements, 320, 128), F32),
            pltpu.VMEM((2, elements, 320, 128), F32),
            pltpu.VMEM((2, 320, 128), F32),
            pltpu.VMEM((12,) + face, F32),
            pltpu.VMEM((2, size) + face, F32),
            pltpu.VMEM((2, size) + face, F32),
            pltpu.VMEM((2, size, 2, 160, 128), BF16),
            pltpu.VMEM((2, depth + 1) + face, F32),
            pltpu.VMEM((2, depth, width) + face, F32),
            pltpu.VMEM((2, depth + 1) + face, F32),
            pltpu.VMEM((2, depth, width) + face, F32),
            pltpu.VMEM((256, 128), F32),
            pltpu.SemaphoreType.DMA((2,)),
            pltpu.SemaphoreType.DMA((2,)),
            pltpu.SemaphoreType.DMA((4, size)),
            pltpu.SemaphoreType.DMA((4, size)),
            pltpu.SemaphoreType.DMA((4, depth, width)),
            pltpu.SemaphoreType.DMA((4, depth, width)),
        ],
        compiler_params=pltpu.CompilerParams(
            vmem_limit_bytes=56 * 1024 * 1024, collective_id=0, has_side_effects=True
        ),
        name="whole",
    )(
        neighbour_kind,
        neighbour_slot,
        hanging_face,
        send_upward,
        send_downward,
        vectors,
        inverse_blocks,
        jnp.transpose(face_jac, (0, 1, 2, 4, 3)).reshape(rows, 80, 5),
        volume_jac.reshape(elements, 3, 5, 320),
        jnp.asarray(mortar_tiles()),
        jnp.asarray(slope_tiles()),
    )


def solution(mesh):
    split_first = lambda rank: P(AXES, *([None] * (rank - 1)))
    return jax.shard_map(
        functools.partial(on_device, mesh.shape["curve"], mesh.shape["colour"]),
        mesh=mesh,
        in_specs=tuple(split_first(r) for r in (3, 3, 5, 5, 2, 2, 2, 1, 1)),
        out_specs=split_first(3),
        check_vma=False,
    )
```

```python
import functools

import jax
import jax.numpy as jnp
import numpy as np
from jax import lax
from jax.experimental import pallas as pl
from jax.experimental.pallas import tpu as pltpu
from jax.sharding import PartitionSpec as P

NP = 4
F32 = jnp.float32
BF16 = jnp.bfloat16
AXES = ("curve", "colour")


def edge_points(edge_count):
    return -np.cos(np.pi * np.arange(edge_count) / (edge_count - 1))


def lagrange_values(edge_nodes, points):
    values = np.ones((len(points), len(edge_nodes)))
    for j in range(len(edge_nodes)):
        for m in range(len(edge_nodes)):
            if m != j:
                values[:, j] = (
                    values[:, j] * (points - edge_nodes[m]) / (edge_nodes[j] - edge_nodes[m])
                )
    return values


def lagrange_slopes(edge_nodes):
    point_count = len(edge_nodes)
    slopes = np.zeros((point_count, point_count))
    for i in range(point_count):
        for j in range(point_count):
            for m in range(point_count):
                if m != j:
                    product = 1.0 / (edge_nodes[j] - edge_nodes[m])
                    for k in range(point_count):
                        if k != j and k != m:
                            product = (
                                product
                                * (edge_nodes[i] - edge_nodes[k])
                                / (edge_nodes[j] - edge_nodes[k])
                            )
                    slopes[i, j] = slopes[i, j] + product
    return slopes


def mortar_tiles():
    edge_nodes = edge_points(NP)
    halves = [
        lagrange_values(edge_nodes, (edge_nodes - 1.0) / 2.0),
        lagrange_values(edge_nodes, (edge_nodes + 1.0) / 2.0),
    ]
    tables = [np.eye(NP * NP)]
    for q in range(4):
        tables.append(np.kron(halves[q // 2], halves[q % 2]))
    return np.tile(np.stack(tables), (1, 5, 15)).astype(np.float32)


def slope_tiles():
    d = 0.25 * lagrange_slopes(edge_points(NP))
    e = np.eye(NP)
    maps = [np.kron(np.kron(d, e), e), np.kron(np.kron(e, d), e), np.kron(np.kron(e, e), d)]
    return np.tile(np.stack(maps), (1, 1, 5)).astype(np.float32)


def split(x):
    high = x.astype(BF16)
    return high, (x - high.astype(F32)).astype(BF16)


def mm(a, b):
    return jnp.dot(a, b, preferred_element_type=F32)


def product(a, b):
    ah, al = split(a)
    bh, bl = split(b)
    return mm(ah, bh) + mm(ah, bl) + mm(al, bh)


def face_values(x, s, tmp):
    last = NP - 1 if s % 2 else 0
    if s < 2:
        return jnp.concatenate([x[pl.ds(f * 64 + last * 16, 16), :] for f in range(5)], axis=0)
    if s < 4:
        for c in range(4):
            tmp[pl.ds(c, 20, stride=4), :] = x[pl.ds(last * 4 + c, 20, stride=16), :]
        return tmp[...]
    return x[pl.ds(last, 80, stride=4), :]


def lift_into(acc, s, value, tmp):
    last = NP - 1 if s % 2 else 0
    if s < 2:
        for f in range(5):
            acc[pl.ds(f * 64 + last * 16, 16), :] += value[f * 16 : f * 16 + 16]
    elif s < 4:
        tmp[...] = value
        for c in range(4):
            acc[pl.ds(last * 4 + c, 20, stride=16), :] += tmp[pl.ds(c, 20, stride=4), :]
    else:
        acc[pl.ds(last, 80, stride=4), :] += value


def stacked(t):
    high, low = split(t)
    return jnp.concatenate([high, low, high], axis=0)


def scan_rounds(count):
    if count == 1:
        return []
    first = min(3, count - 1)
    rounds, cover = [list(range(1, first + 1))], first
    while cover < count - 1:
        radix = 4 if cover * 3 < count - 1 else (3 if cover * 2 < count - 1 else 2)
        rounds.append([cover * i for i in range(1, radix)])
        cover *= radix
    return rounds


def group_size(count):
    return next(size for size in (8, 4, 2, 1) if count % size == 0)


def kernel(
    curve_size,
    colour_size,
    kind_ref,
    slot_ref,
    hang_ref,
    up_ref,
    down_ref,
    u_ref,
    inv_ref,
    jac_ref,
    vjac_ref,
    mortar_ref,
    slope_ref,
    out_ref,
    maps,
    traces,
    leaving,
    near,
    table_u,
    table_wf,
    table_wb,
    table_y,
    table_z,
    image,
    wide_f,
    wide_b,
    lowered,
    solved,
    acc,
    tmp,
    group_m,
    group_v,
    factors,
    state_m,
    recv_m,
    state_v,
    recv_v,
    both,
    near_send,
    near_recv,
    group_send,
    group_recv,
    chain_send,
    chain_recv,
):
    elements = u_ref.shape[0]
    rows = elements * 6
    count = curve_size * colour_size
    size = group_size(count)
    rounds = scan_rounds(count // size)
    me = lax.axis_index("curve") * colour_size + lax.axis_index("colour")
    place = lax.rem(me, size)
    first = me - place

    def coordinates(other):
        other = lax.rem(other + count, count)
        return (other // colour_size, lax.rem(other, colour_size))

    barrier = pltpu.get_barrier_semaphore()
    greeted = jnp.int32(size - 1)

    def greet(other):
        pl.semaphore_signal(
            barrier, inc=1, device_id=coordinates(other), device_id_type=pl.DeviceIdType.MESH
        )

    def peer(i):
        return first + lax.rem(place + i, size)

    for i in range(1, size):
        greet(peer(i))
    distant = [
        (me + 1, (place == size - 1) & (me + 1 < count)),
        (me - 1, (place == 0) & (me > 0)),
    ]
    for offset in sorted({o for r in rounds for o in r}):
        if offset * size > 1:
            distant.append((me + offset * size, me + offset * size < count))
            distant.append((me - offset * size, me >= offset * size))
    for other, there in distant:
        greeted = greeted + there.astype(jnp.int32)

        @pl.when(there)
        def _(other=other):
            greet(other)

    sent = []

    def remote(source, target, send, recv, other, has_to, has_from):
        copy = pltpu.make_async_remote_copy(
            src_ref=source,
            dst_ref=target,
            send_sem=send,
            recv_sem=recv,
            device_id=coordinates(other),
            device_id_type=pl.DeviceIdType.MESH,
        )

        @pl.when(has_to)
        def _():
            copy.start()

        @pl.when(jnp.logical_not(has_from))
        def _():
            target[...] = jnp.zeros(target.shape, F32)

        sent.append((copy, has_to))
        return copy, has_from

    def arrive(copies):
        for copy, has_from in copies:

            @pl.when(has_from)
            def _(copy=copy):
                copy.wait_recv()

    lane = lax.broadcasted_iota(jnp.int32, (80, 240), 1)
    eye = (
        lax.broadcasted_iota(jnp.int32, (80, 128), 0)
        == lax.broadcasted_iota(jnp.int32, (80, 128), 1)
    ).astype(F32)
    none = jnp.zeros((240, 128), BF16)
    spread = (
        lax.rem(lax.broadcasted_iota(jnp.int32, (5, 240), 1), 80) // 16
        == lax.broadcasted_iota(jnp.int32, (5, 240), 0)
    ).astype(BF16)
    for j in range(elements):
        for s in range(6):
            t = face_values(u_ref.at[j], s, tmp.at[s])
            traces[j * 6 + s] = t
            table_u[j * 6 + s] = stacked(t)
    table_u[rows] = none
    leaving[0] = traces[up_ref[0]]
    leaving[1] = traces[down_ref[0]]
    pl.semaphore_wait(barrier, greeted)
    after, before = me + 1 < count, me > 0
    near_copies = [
        remote(leaving.at[0], near.at[0], near_send.at[0], near_recv.at[0], me + 1, after, before),
        remote(leaving.at[1], near.at[1], near_send.at[1], near_recv.at[1], me - 1, before, after),
    ]
    for j in range(elements):
        for s in range(6):
            high, low = split(jac_ref[j * 6 + s])
            wide = (mm(high, spread) + mm(low, spread)) * mortar_ref[hang_ref[j, s]]
            high = wide.astype(BF16).astype(F32)
            maps[j * 6 + s] = jnp.where(lane < 160, high, wide - high).astype(BF16)

    def step(j, backward, table, remote_row, empty_row, accs, tmps, own, dests):
        groups = len(dests)
        for g in range(groups):
            acc[accs + g] = jnp.zeros((320, 128), F32)
        for s in range(6):
            kind, slot = kind_ref[j, s], slot_ref[j, s]
            inside = slot >= 6 * (j + 1) if backward else slot < 6 * j
            row = jnp.where(kind == (3 if backward else 2), remote_row, empty_row)
            row = jnp.where((kind == 1) & inside, slot, row)
            value = mm(maps[j * 6 + s], table[row])
            for g in range(groups):
                lift_into(
                    acc.at[accs + g], s, value[:, g * 128 : g * 128 + 128], tmp.at[tmps + 6 * g + s]
                )
        if backward:
            right = [acc[accs + g] for g in range(groups)]
        else:
            right = [own[g] - acc[accs + g] for g in range(groups)]
        high, low = split(jnp.concatenate(right, axis=1) if groups > 1 else right[0])
        value = mm(inv_ref[j], high) + mm(inv_ref[j], low)
        for g in range(groups):
            part = value[:, g * 128 : g * 128 + 128]
            dests[g][...] = own[g] - part if backward else part
            for s in range(6):
                table[j * 6 + s, :, g * 128 : g * 128 + 128] = stacked(
                    face_values(dests[g], s, tmp.at[tmps + 6 * g + s])
                )

    def outgoing(table, which):
        out = table[which]
        return out[:80].astype(F32) + out[80:160].astype(F32)

    def share(buffer, kind):
        copies = []
        for i in range(1, size):
            copy = pltpu.make_async_remote_copy(
                src_ref=buffer.at[place],
                dst_ref=buffer.at[place],
                send_sem=group_send.at[kind, i],
                recv_sem=group_recv.at[kind, place],
                device_id=coordinates(peer(i)),
                device_id_type=pl.DeviceIdType.MESH,
            )
            copy.start()
            sent.append((copy, None))
        for i in range(1, size):
            other = lax.rem(place + i, size)
            copies.append(
                pltpu.make_async_remote_copy(
                    src_ref=buffer.at[other],
                    dst_ref=buffer.at[other],
                    send_sem=group_send.at[kind, i],
                    recv_sem=group_recv.at[kind, other],
                    device_id=coordinates(peer(i)),
                    device_id_type=pl.DeviceIdType.MESH,
                )
            )
        return copies

    unit = stacked(eye)
    for table in (table_wf, table_wb):
        table[rows] = unit
        table[rows + 1] = none
    zero = jnp.zeros((320, 128), F32)
    for p in range(elements):
        step(p, False, table_wf, rows, rows + 1, 0, 0, [zero], [wide_f.at[p]])
    group_m[0, place] = outgoing(table_wf, up_ref[0])
    shared_mf = share(group_m.at[0], 0)

    arrive(near_copies)
    table_u[rows + 1] = stacked(near[0])
    table_u[rows + 2] = stacked(near[1])
    for j in range(elements):
        parts = []
        for f in range(5):
            part = slope_ref[0] * vjac_ref[j, 0, f : f + 1, :]
            for t in range(1, 3):
                part = part + slope_ref[t] * vjac_ref[j, t, f : f + 1, :]
            parts.append(part)
        volume = jnp.concatenate(parts, axis=0)
        image[j] = u_ref[j] + product(volume, u_ref[j])
        for s in range(6):
            kind, slot = kind_ref[j, s], slot_ref[j, s]
            row = jnp.where(kind == 1, slot, jnp.where(kind == 0, rows, rows + kind - 1))
            lift_into(image.at[j], s, mm(maps[j * 6 + s], table_u[row]), tmp.at[s])
    table_y[rows] = none
    for j in range(elements):
        step(j, False, table_y, rows, rows, 0, 0, [image[j]], [lowered.at[j]])
    group_v[0, place] = outgoing(table_y, up_ref[0])
    shared_f = share(group_v.at[0], 2)

    for p in range(elements):
        step(elements - 1 - p, True, table_wb, rows, rows + 1, 1, 6, [zero], [wide_b.at[elements - 1 - p]])
    group_m[1, place] = outgoing(table_wb, down_ref[0])
    shared_mb = share(group_m.at[1], 1)

    def pass_on(way, k, i, source, target, kind):
        offset = rounds[k][i] * size
        below, above = me >= offset, me + offset < count
        return remote(
            source,
            target,
            chain_send.at[kind, k, i],
            chain_recv.at[kind, k, i],
            me - offset if way else me + offset,
            below if way else above,
            above if way else below,
        )

    def start_m(way, k):
        return [
            pass_on(way, k, i, state_m.at[way, k], recv_m.at[way, k, i], way)
            for i in range(len(rounds[k]))
        ]

    def chain_maps(way, copies):
        for copy in copies:
            copy.wait_recv()
        chain = jnp.concatenate([eye, eye], axis=0)
        for index in range(size):
            e = index if way else size - 1 - index
            mine = place < e if way else place > e
            high, low = split(jnp.concatenate([jnp.where(mine, chain[:80], 0.0), chain[80:]], 0))
            factors[way, e, 0] = high
            factors[way, e, 1] = low
            following = product(chain[:, :80], group_m[way, e])
            chain = jnp.concatenate([jnp.where(mine, following[:80], eye), following[80:]], 0)
        state_m[way, 0] = chain[80:]
        return chain[:80], start_m(way, 0) if rounds else []

    def finish_maps(way, pending):
        for k in range(len(rounds)):
            arrive(pending)
            if k + 1 < len(rounds):
                factor = [recv_m[way, k, i] for i in range(len(rounds[k]))]
                if k > 0:
                    factor = [state_m[way, k]] + factor
                total = factor[-1]
                for item in factor[-2::-1]:
                    total = product(item[:, :80], total)
                state_m[way, k + 1] = total
                pending = start_m(way, k + 1)

    enter_f, pending_f = chain_maps(0, shared_mf)

    table_z[rows, :, 0:128] = none
    table_z[rows, :, 128:256] = none
    for p in range(elements):
        q = elements - 1 - p
        step(
            q,
            True,
            table_z,
            rows,
            rows,
            0,
            0,
            [lowered[q], wide_f[q]],
            [solved.at[0, q], solved.at[1, q]],
        )
    back = outgoing(table_z, down_ref[0])

    def weighted(way, half):
        total = jnp.zeros((80, 128), F32)
        for e in range(size):
            high, low = split(group_v[way, e])
            fh = factors[way, e, 0, half : half + 80, :80]
            fl = factors[way, e, 1, half : half + 80, :80]
            total = total + mm(fh, high) + mm(fh, low) + mm(fl, high)
        return total

    def start_v(way, k):
        return [
            pass_on(way, k, i, state_v.at[way, k], recv_v.at[way, k, i], 2 + way)
            for i in range(len(rounds[k]))
        ]

    def start_scan(way, copies):
        for copy in copies:
            copy.wait_recv()
        if not rounds:
            return weighted(way, 0), []
        state_v[way, 0] = weighted(way, 80)
        moving = start_v(way, 0)
        return weighted(way, 0), moving

    def finish_scan(way, own, moving, enter):
        if not rounds:
            return own
        for k, offsets in enumerate(rounds):
            arrive(moving)
            links = [(recv_v.at[way, k, i], recv_m.at[way, k, i]) for i in range(len(offsets))]
            if k > 0:
                links = [(state_v.at[way, k], state_m.at[way, k])] + links
            value = links[-1][0][...]
            for term, factor in links[-2::-1]:
                value = term[...] + product(factor[:, :80], value)
            state_v[way, k + 1] = value
            if k + 1 < len(rounds):
                moving = start_v(way, k + 1)
        return own + product(enter[:, :80], state_v[way, len(rounds)])

    both[...] = jnp.zeros(both.shape, F32)
    own, moving = start_scan(0, shared_f)
    enter_b, pending_b = chain_maps(1, shared_mb)
    finish_maps(0, pending_f)
    incoming = finish_scan(0, own, moving, enter_f)
    group_v[1, place] = back[:, :128] + product(back[:, 128:208], incoming)
    shared_b = share(group_v.at[1], 3)
    both[0:80] = incoming
    finish_maps(1, pending_b)
    own, moving = start_scan(1, shared_b)
    both[128:208] = finish_scan(1, own, moving, enter_b)

    high, low = split(both[...])
    for j in range(elements):
        wh, wl = split(jnp.concatenate([solved[1, j], wide_b[j]], axis=1))
        out_ref[j] = solved[0, j] + mm(wh, high) + mm(wh, low) + mm(wl, high)
    for copy, has_to in sent:
        if has_to is None:
            copy.wait_send()
        else:

            @pl.when(has_to)
            def _(copy=copy):
                copy.wait_send()


def on_device(
    curve_size,
    colour_size,
    vectors,
    inverse_blocks,
    face_jac,
    volume_jac,
    neighbour_kind,
    neighbour_slot,
    hanging_face,
    send_upward,
    send_downward,
):
    elements = vectors.shape[0]
    rows = elements * 6
    count = curve_size * colour_size
    size = group_size(count)
    rounds = scan_rounds(count // size)
    depth = max(len(rounds), 1)
    width = max([len(r) for r in rounds] + [1])
    smem = pl.BlockSpec(memory_space=pltpu.SMEM)
    vmem = pl.BlockSpec(memory_space=pltpu.VMEM)
    face = (80, 128)
    return pl.pallas_call(
        functools.partial(kernel, curve_size, colour_size),
        out_shape=jax.ShapeDtypeStruct(vectors.shape, F32),
        in_specs=[smem] * 5 + [vmem] * 6,
        out_specs=vmem,
        scratch_shapes=[
            pltpu.VMEM((rows, 80, 240), BF16),
            pltpu.VMEM((rows,) + face, F32),
            pltpu.VMEM((2,) + face, F32),
            pltpu.VMEM((2,) + face, F32),
            pltpu.VMEM((rows + 3, 240, 128), BF16),
            pltpu.VMEM((rows + 2, 240, 128), BF16),
            pltpu.VMEM((rows + 2, 240, 128), BF16),
            pltpu.VMEM((rows + 1, 240, 128), BF16),
            pltpu.VMEM((rows + 1, 240, 256), BF16),
            pltpu.VMEM((elements, 320, 128), F32),
            pltpu.VMEM((elements, 320, 128), F32),
            pltpu.VMEM((elements, 320, 128), F32),
            pltpu.VMEM((elements, 320, 128), F32),
            pltpu.VMEM((2, elements, 320, 128), F32),
            pltpu.VMEM((2, 320, 128), F32),
            pltpu.VMEM((12,) + face, F32),
            pltpu.VMEM((2, size) + face, F32),
            pltpu.VMEM((2, size) + face, F32),
            pltpu.VMEM((2, size, 2, 160, 128), BF16),
            pltpu.VMEM((2, depth + 1) + face, F32),
            pltpu.VMEM((2, depth, width) + face, F32),
            pltpu.VMEM((2, depth + 1) + face, F32),
            pltpu.VMEM((2, depth, width) + face, F32),
            pltpu.VMEM((256, 128), F32),
            pltpu.SemaphoreType.DMA((2,)),
            pltpu.SemaphoreType.DMA((2,)),
            pltpu.SemaphoreType.DMA((4, size)),
            pltpu.SemaphoreType.DMA((4, size)),
            pltpu.SemaphoreType.DMA((4, depth, width)),
            pltpu.SemaphoreType.DMA((4, depth, width)),
        ],
        compiler_params=pltpu.CompilerParams(
            vmem_limit_bytes=56 * 1024 * 1024, collective_id=0, has_side_effects=True
        ),
        name="whole",
    )(
        neighbour_kind,
        neighbour_slot,
        hanging_face,
        send_upward,
        send_downward,
        vectors,
        inverse_blocks,
        jnp.transpose(face_jac, (0, 1, 2, 4, 3)).reshape(rows, 80, 5),
        volume_jac.reshape(elements, 3, 5, 320),
        jnp.asarray(mortar_tiles()),
        jnp.asarray(slope_tiles()),
    )


def solution(mesh):
    split_first = lambda rank: P(AXES, *([None] * (rank - 1)))
    return jax.shard_map(
        functools.partial(on_device, mesh.shape["curve"], mesh.shape["colour"]),
        mesh=mesh,
        in_specs=tuple(split_first(r) for r in (3, 3, 5, 5, 2, 2, 2, 1, 1)),
        out_specs=split_first(3),
        check_vma=False,
    )
```

```python
import functools

import jax
import jax.numpy as jnp
import numpy as np
from jax import lax
from jax.experimental import pallas as pl
from jax.experimental.pallas import tpu as pltpu
from jax.sharding import PartitionSpec as P

NP = 4
F32 = jnp.float32
BF16 = jnp.bfloat16
AXES = ("curve", "colour")


def edge_points(edge_count):
    return -np.cos(np.pi * np.arange(edge_count) / (edge_count - 1))


def lagrange_values(edge_nodes, points):
    values = np.ones((len(points), len(edge_nodes)))
    for j in range(len(edge_nodes)):
        for m in range(len(edge_nodes)):
            if m != j:
                values[:, j] = (
                    values[:, j] * (points - edge_nodes[m]) / (edge_nodes[j] - edge_nodes[m])
                )
    return values


def lagrange_slopes(edge_nodes):
    point_count = len(edge_nodes)
    slopes = np.zeros((point_count, point_count))
    for i in range(point_count):
        for j in range(point_count):
            for m in range(point_count):
                if m != j:
                    product = 1.0 / (edge_nodes[j] - edge_nodes[m])
                    for k in range(point_count):
                        if k != j and k != m:
                            product = (
                                product
                                * (edge_nodes[i] - edge_nodes[k])
                                / (edge_nodes[j] - edge_nodes[k])
                            )
                    slopes[i, j] = slopes[i, j] + product
    return slopes


def mortar_tiles():
    edge_nodes = edge_points(NP)
    halves = [
        lagrange_values(edge_nodes, (edge_nodes - 1.0) / 2.0),
        lagrange_values(edge_nodes, (edge_nodes + 1.0) / 2.0),
    ]
    tables = [np.eye(NP * NP)]
    for q in range(4):
        tables.append(np.kron(halves[q // 2], halves[q % 2]))
    return np.tile(np.stack(tables), (1, 5, 15)).astype(np.float32)


def slope_tiles():
    d = 0.25 * lagrange_slopes(edge_points(NP))
    e = np.eye(NP)
    maps = [np.kron(np.kron(d, e), e), np.kron(np.kron(e, d), e), np.kron(np.kron(e, e), d)]
    return np.tile(np.stack(maps), (1, 1, 5)).astype(np.float32)


def split(x):
    high = x.astype(BF16)
    return high, (x - high.astype(F32)).astype(BF16)


def mm(a, b):
    return jnp.dot(a, b, preferred_element_type=F32)


def product(a, b):
    ah, al = split(a)
    bh, bl = split(b)
    return mm(ah, bh) + mm(ah, bl) + mm(al, bh)


def face_values(x, s, tmp):
    last = NP - 1 if s % 2 else 0
    if s < 2:
        return jnp.concatenate([x[pl.ds(f * 64 + last * 16, 16), :] for f in range(5)], axis=0)
    if s < 4:
        for c in range(4):
            tmp[pl.ds(c, 20, stride=4), :] = x[pl.ds(last * 4 + c, 20, stride=16), :]
        return tmp[...]
    return x[pl.ds(last, 80, stride=4), :]


def lift_into(acc, s, value, tmp):
    last = NP - 1 if s % 2 else 0
    if s < 2:
        for f in range(5):
            acc[pl.ds(f * 64 + last * 16, 16), :] += value[f * 16 : f * 16 + 16]
    elif s < 4:
        tmp[...] = value
        for c in range(4):
            acc[pl.ds(last * 4 + c, 20, stride=16), :] += tmp[pl.ds(c, 20, stride=4), :]
    else:
        acc[pl.ds(last, 80, stride=4), :] += value


def stacked(t):
    high, low = split(t)
    return jnp.concatenate([high, low, high], axis=0)


def scan_rounds(count):
    if count == 1:
        return []
    first = min(3, count - 1)
    rounds, cover = [list(range(1, first + 1))], first
    while cover < count - 1:
        radix = 4 if cover * 3 < count - 1 else (3 if cover * 2 < count - 1 else 2)
        rounds.append([cover * i for i in range(1, radix)])
        cover *= radix
    return rounds


def group_size(count):
    return next(size for size in (8, 4, 2, 1) if count % size == 0)


def kernel(
    curve_size,
    colour_size,
    kind_ref,
    slot_ref,
    hang_ref,
    up_ref,
    down_ref,
    u_ref,
    inv_ref,
    jac_ref,
    vjac_ref,
    mortar_ref,
    slope_ref,
    out_ref,
    maps,
    traces,
    leaving,
    near,
    table_u,
    table_wf,
    table_wb,
    table_y,
    table_z,
    image,
    wide_f,
    wide_b,
    lowered,
    solved,
    acc,
    tmp,
    group_m,
    group_v,
    factors,
    state_m,
    recv_m,
    state_v,
    recv_v,
    both,
    near_send,
    near_recv,
    group_send,
    group_recv,
    chain_send,
    chain_recv,
):
    elements = u_ref.shape[0]
    rows = elements * 6
    count = curve_size * colour_size
    size = group_size(count)
    rounds = scan_rounds(count // size)
    me = lax.axis_index("curve") * colour_size + lax.axis_index("colour")
    place = lax.rem(me, size)
    first = me - place

    def coordinates(other):
        other = lax.rem(other + count, count)
        return (other // colour_size, lax.rem(other, colour_size))

    barrier = pltpu.get_barrier_semaphore()
    greeted = jnp.int32(size - 1)

    def greet(other):
        pl.semaphore_signal(
            barrier, inc=1, device_id=coordinates(other), device_id_type=pl.DeviceIdType.MESH
        )

    def peer(i):
        return first + lax.rem(place + i, size)

    for i in range(1, size):
        greet(peer(i))
    distant = [
        (me + 1, (place == size - 1) & (me + 1 < count)),
        (me - 1, (place == 0) & (me > 0)),
    ]
    for offset in sorted({o for r in rounds for o in r}):
        if offset * size > 1:
            distant.append((me + offset * size, me + offset * size < count))
            distant.append((me - offset * size, me >= offset * size))
    for other, there in distant:
        greeted = greeted + there.astype(jnp.int32)

        @pl.when(there)
        def _(other=other):
            greet(other)

    sent = []

    def remote(source, target, send, recv, other, has_to, has_from):
        copy = pltpu.make_async_remote_copy(
            src_ref=source,
            dst_ref=target,
            send_sem=send,
            recv_sem=recv,
            device_id=coordinates(other),
            device_id_type=pl.DeviceIdType.MESH,
        )

        @pl.when(has_to)
        def _():
            copy.start()

        @pl.when(jnp.logical_not(has_from))
        def _():
            target[...] = jnp.zeros(target.shape, F32)

        sent.append((copy, has_to))
        return copy, has_from

    def arrive(copies):
        for copy, has_from in copies:

            @pl.when(has_from)
            def _(copy=copy):
                copy.wait_recv()

    lane = lax.broadcasted_iota(jnp.int32, (80, 240), 1)
    eye = (
        lax.broadcasted_iota(jnp.int32, (80, 128), 0)
        == lax.broadcasted_iota(jnp.int32, (80, 128), 1)
    ).astype(F32)
    none = jnp.zeros((240, 128), BF16)
    spread = (
        lax.rem(lax.broadcasted_iota(jnp.int32, (5, 240), 1), 80) // 16
        == lax.broadcasted_iota(jnp.int32, (5, 240), 0)
    ).astype(BF16)
    for j in range(elements):
        for s in range(6):
            t = face_values(u_ref.at[j], s, tmp.at[s])
            traces[j * 6 + s] = t
            table_u[j * 6 + s] = stacked(t)
    table_u[rows] = none
    leaving[0] = traces[up_ref[0]]
    leaving[1] = traces[down_ref[0]]
    for j in range(elements):
        for s in range(6):
            high, low = split(jac_ref[j * 6 + s])
            wide = (mm(high, spread) + mm(low, spread)) * mortar_ref[hang_ref[j, s]]
            high = wide.astype(BF16).astype(F32)
            maps[j * 6 + s] = jnp.where(lane < 160, high, wide - high).astype(BF16)
    pl.semaphore_wait(barrier, greeted)
    after, before = me + 1 < count, me > 0
    near_copies = [
        remote(leaving.at[0], near.at[0], near_send.at[0], near_recv.at[0], me + 1, after, before),
        remote(leaving.at[1], near.at[1], near_send.at[1], near_recv.at[1], me - 1, before, after),
    ]

    def step(j, backward, table, remote_row, empty_row, accs, tmps, own, dests):
        groups = len(dests)
        for g in range(groups):
            acc[accs + g] = jnp.zeros((320, 128), F32)
        for s in range(6):
            kind, slot = kind_ref[j, s], slot_ref[j, s]
            inside = slot >= 6 * (j + 1) if backward else slot < 6 * j
            row = jnp.where(kind == (3 if backward else 2), remote_row, empty_row)
            row = jnp.where((kind == 1) & inside, slot, row)
            value = mm(maps[j * 6 + s], table[row])
            for g in range(groups):
                lift_into(
                    acc.at[accs + g], s, value[:, g * 128 : g * 128 + 128], tmp.at[tmps + 6 * g + s]
                )
        if backward:
            right = [acc[accs + g] for g in range(groups)]
        else:
            right = [own[g] - acc[accs + g] for g in range(groups)]
        high, low = split(jnp.concatenate(right, axis=1) if groups > 1 else right[0])
        value = mm(inv_ref[j], high) + mm(inv_ref[j], low)
        for g in range(groups):
            part = value[:, g * 128 : g * 128 + 128]
            dests[g][...] = own[g] - part if backward else part
            for s in range(6):
                table[j * 6 + s, :, g * 128 : g * 128 + 128] = stacked(
                    face_values(dests[g], s, tmp.at[tmps + 6 * g + s])
                )

    def outgoing(table, which):
        out = table[which]
        return out[:80].astype(F32) + out[80:160].astype(F32)

    def share(buffer, kind):
        copies = []
        for i in range(1, size):
            copy = pltpu.make_async_remote_copy(
                src_ref=buffer.at[place],
                dst_ref=buffer.at[place],
                send_sem=group_send.at[kind, i],
                recv_sem=group_recv.at[kind, place],
                device_id=coordinates(peer(i)),
                device_id_type=pl.DeviceIdType.MESH,
            )
            copy.start()
            sent.append((copy, None))
        for i in range(1, size):
            other = lax.rem(place + i, size)
            copies.append(
                pltpu.make_async_remote_copy(
                    src_ref=buffer.at[other],
                    dst_ref=buffer.at[other],
                    send_sem=group_send.at[kind, i],
                    recv_sem=group_recv.at[kind, other],
                    device_id=coordinates(peer(i)),
                    device_id_type=pl.DeviceIdType.MESH,
                )
            )
        return copies

    unit = stacked(eye)
    for table in (table_wf, table_wb):
        table[rows] = unit
        table[rows + 1] = none
    zero = jnp.zeros((320, 128), F32)
    for p in range(elements):
        step(p, False, table_wf, rows, rows + 1, 0, 0, [zero], [wide_f.at[p]])
    group_m[0, place] = outgoing(table_wf, up_ref[0])
    shared_mf = share(group_m.at[0], 0)

    for j in range(elements):
        parts = []
        for f in range(5):
            part = slope_ref[0] * vjac_ref[j, 0, f : f + 1, :]
            for t in range(1, 3):
                part = part + slope_ref[t] * vjac_ref[j, t, f : f + 1, :]
            parts.append(part)
        volume = jnp.concatenate(parts, axis=0)
        image[j] = u_ref[j] + product(volume, u_ref[j])
    arrive(near_copies)
    table_u[rows + 1] = stacked(near[0])
    table_u[rows + 2] = stacked(near[1])
    for j in range(elements):
        for s in range(6):
            kind, slot = kind_ref[j, s], slot_ref[j, s]
            row = jnp.where(kind == 1, slot, jnp.where(kind == 0, rows, rows + kind - 1))
            lift_into(image.at[j], s, mm(maps[j * 6 + s], table_u[row]), tmp.at[s])
    table_y[rows] = none
    for j in range(elements):
        step(j, False, table_y, rows, rows, 0, 0, [image[j]], [lowered.at[j]])
    group_v[0, place] = outgoing(table_y, up_ref[0])
    shared_f = share(group_v.at[0], 2)

    for p in range(elements):
        step(elements - 1 - p, True, table_wb, rows, rows + 1, 1, 6, [zero], [wide_b.at[elements - 1 - p]])
    group_m[1, place] = outgoing(table_wb, down_ref[0])
    shared_mb = share(group_m.at[1], 1)

    def pass_on(way, k, i, source, target, kind):
        offset = rounds[k][i] * size
        below, above = me >= offset, me + offset < count
        return remote(
            source,
            target,
            chain_send.at[kind, k, i],
            chain_recv.at[kind, k, i],
            me - offset if way else me + offset,
            below if way else above,
            above if way else below,
        )

    def start_m(way, k):
        return [
            pass_on(way, k, i, state_m.at[way, k], recv_m.at[way, k, i], way)
            for i in range(len(rounds[k]))
        ]

    def chain_maps(way, copies):
        for copy in copies:
            copy.wait_recv()
        chain = jnp.concatenate([eye, eye], axis=0)
        for index in range(size):
            e = index if way else size - 1 - index
            mine = place < e if way else place > e
            high, low = split(jnp.concatenate([jnp.where(mine, chain[:80], 0.0), chain[80:]], 0))
            factors[way, e, 0] = high
            factors[way, e, 1] = low
            following = product(chain[:, :80], group_m[way, e])
            chain = jnp.concatenate([jnp.where(mine, following[:80], eye), following[80:]], 0)
        state_m[way, 0] = chain[80:]
        return chain[:80], start_m(way, 0) if rounds else []

    def finish_maps(way, pending):
        for k in range(len(rounds)):
            arrive(pending)
            if k + 1 < len(rounds):
                factor = [recv_m[way, k, i] for i in range(len(rounds[k]))]
                if k > 0:
                    factor = [state_m[way, k]] + factor
                total = factor[-1]
                for item in factor[-2::-1]:
                    total = product(item[:, :80], total)
                state_m[way, k + 1] = total
                pending = start_m(way, k + 1)

    enter_f, pending_f = chain_maps(0, shared_mf)

    table_z[rows, :, 0:128] = none
    table_z[rows, :, 128:256] = none
    for p in range(elements):
        q = elements - 1 - p
        step(
            q,
            True,
            table_z,
            rows,
            rows,
            0,
            0,
            [lowered[q], wide_f[q]],
            [solved.at[0, q], solved.at[1, q]],
        )
    back = outgoing(table_z, down_ref[0])

    def weighted(way, half):
        total = jnp.zeros((80, 128), F32)
        for e in range(size):
            high, low = split(group_v[way, e])
            fh = factors[way, e, 0, half : half + 80, :80]
            fl = factors[way, e, 1, half : half + 80, :80]
            total = total + mm(fh, high) + mm(fh, low) + mm(fl, high)
        return total

    def start_v(way, k):
        return [
            pass_on(way, k, i, state_v.at[way, k], recv_v.at[way, k, i], 2 + way)
            for i in range(len(rounds[k]))
        ]

    def start_scan(way, copies):
        for copy in copies:
            copy.wait_recv()
        if not rounds:
            return weighted(way, 0), []
        state_v[way, 0] = weighted(way, 80)
        moving = start_v(way, 0)
        return weighted(way, 0), moving

    def finish_scan(way, own, moving, enter):
        if not rounds:
            return own
        for k, offsets in enumerate(rounds):
            arrive(moving)
            links = [(recv_v.at[way, k, i], recv_m.at[way, k, i]) for i in range(len(offsets))]
            if k > 0:
                links = [(state_v.at[way, k], state_m.at[way, k])] + links
            value = links[-1][0][...]
            for term, factor in links[-2::-1]:
                value = term[...] + product(factor[:, :80], value)
            state_v[way, k + 1] = value
            if k + 1 < len(rounds):
                moving = start_v(way, k + 1)
        return own + product(enter[:, :80], state_v[way, len(rounds)])

    both[...] = jnp.zeros(both.shape, F32)
    own, moving = start_scan(0, shared_f)
    enter_b, pending_b = chain_maps(1, shared_mb)
    finish_maps(0, pending_f)
    incoming = finish_scan(0, own, moving, enter_f)
    group_v[1, place] = back[:, :128] + product(back[:, 128:208], incoming)
    shared_b = share(group_v.at[1], 3)
    both[0:80] = incoming
    finish_maps(1, pending_b)
    own, moving = start_scan(1, shared_b)
    both[128:208] = finish_scan(1, own, moving, enter_b)

    high, low = split(both[...])
    for j in range(elements):
        wh, wl = split(jnp.concatenate([solved[1, j], wide_b[j]], axis=1))
        out_ref[j] = solved[0, j] + mm(wh, high) + mm(wh, low) + mm(wl, high)
    for copy, has_to in sent:
        if has_to is None:
            copy.wait_send()
        else:

            @pl.when(has_to)
            def _(copy=copy):
                copy.wait_send()


def on_device(
    curve_size,
    colour_size,
    vectors,
    inverse_blocks,
    face_jac,
    volume_jac,
    neighbour_kind,
    neighbour_slot,
    hanging_face,
    send_upward,
    send_downward,
):
    elements = vectors.shape[0]
    rows = elements * 6
    count = curve_size * colour_size
    size = group_size(count)
    rounds = scan_rounds(count // size)
    depth = max(len(rounds), 1)
    width = max([len(r) for r in rounds] + [1])
    smem = pl.BlockSpec(memory_space=pltpu.SMEM)
    vmem = pl.BlockSpec(memory_space=pltpu.VMEM)
    face = (80, 128)
    return pl.pallas_call(
        functools.partial(kernel, curve_size, colour_size),
        out_shape=jax.ShapeDtypeStruct(vectors.shape, F32),
        in_specs=[smem] * 5 + [vmem] * 6,
        out_specs=vmem,
        scratch_shapes=[
            pltpu.VMEM((rows, 80, 240), BF16),
            pltpu.VMEM((rows,) + face, F32),
            pltpu.VMEM((2,) + face, F32),
            pltpu.VMEM((2,) + face, F32),
            pltpu.VMEM((rows + 3, 240, 128), BF16),
            pltpu.VMEM((rows + 2, 240, 128), BF16),
            pltpu.VMEM((rows + 2, 240, 128), BF16),
            pltpu.VMEM((rows + 1, 240, 128), BF16),
            pltpu.VMEM((rows + 1, 240, 256), BF16),
            pltpu.VMEM((elements, 320, 128), F32),
            pltpu.VMEM((elements, 320, 128), F32),
            pltpu.VMEM((elements, 320, 128), F32),
            pltpu.VMEM((elements, 320, 128), F32),
            pltpu.VMEM((2, elements, 320, 128), F32),
            pltpu.VMEM((2, 320, 128), F32),
            pltpu.VMEM((12,) + face, F32),
            pltpu.VMEM((2, size) + face, F32),
            pltpu.VMEM((2, size) + face, F32),
            pltpu.VMEM((2, size, 2, 160, 128), BF16),
            pltpu.VMEM((2, depth + 1) + face, F32),
            pltpu.VMEM((2, depth, width) + face, F32),
            pltpu.VMEM((2, depth + 1) + face, F32),
            pltpu.VMEM((2, depth, width) + face, F32),
            pltpu.VMEM((256, 128), F32),
            pltpu.SemaphoreType.DMA((2,)),
            pltpu.SemaphoreType.DMA((2,)),
            pltpu.SemaphoreType.DMA((4, size)),
            pltpu.SemaphoreType.DMA((4, size)),
            pltpu.SemaphoreType.DMA((4, depth, width)),
            pltpu.SemaphoreType.DMA((4, depth, width)),
        ],
        compiler_params=pltpu.CompilerParams(
            vmem_limit_bytes=56 * 1024 * 1024, collective_id=0, has_side_effects=True
        ),
        name="whole",
    )(
        neighbour_kind,
        neighbour_slot,
        hanging_face,
        send_upward,
        send_downward,
        vectors,
        inverse_blocks,
        jnp.transpose(face_jac, (0, 1, 2, 4, 3)).reshape(rows, 80, 5),
        volume_jac.reshape(elements, 3, 5, 320),
        jnp.asarray(mortar_tiles()),
        jnp.asarray(slope_tiles()),
    )


def solution(mesh):
    split_first = lambda rank: P(AXES, *([None] * (rank - 1)))
    return jax.shard_map(
        functools.partial(on_device, mesh.shape["curve"], mesh.shape["colour"]),
        mesh=mesh,
        in_specs=tuple(split_first(r) for r in (3, 3, 5, 5, 2, 2, 2, 1, 1)),
        out_specs=split_first(3),
        check_vma=False,
    )
```
